32 devices in a mesh: groups: 2 (over y), blk: 4 (over x, core), layer: 4 (over z).
Axes of the slice: x: 2, y: 2, z: 4, core: 2. Of those that a mesh axis runs over, the one named last changes fastest.
Arguments:
- train_grads: bfloat16 [2048, 4, 4096], P(('groups', 'blk'), 'layer'), parts along dimension 0, may hold values from -6 to 6
- query_grads: bfloat16 [2048, 4, 4096], P(('groups', 'blk'), 'layer'), parts along dimension 0, may hold values from -6 to 6
- eigenvalues: float32 [4, 4096], P('layer'), may hold values from 0.02 to 2
- order: int32 [6, 256], P('groups'), parts along dimension 0, may hold values from 0 to 255, each once within a row
Outputs:
- scores: float32 [3, 256, 2048], P(None, 'layer', ('groups', 'blk')), parts along dimension 2
The draws below stay inside these ranges and needn't reach their ends.
There are 2 independent parts, one for each index of `groups`. The reference program is written for one: setup_inputs(seed, part) draws one part's arguments, and reference() takes and returns one part's arrays. A program takes and returns all parts, laid end to end along the dimension named above; an argument that names none is the same for every part. Nothing has to cross between parts.
Inputs may be any that keep to these rules, and one draw needn't show every extreme that they name: Each row of order is a permutation of 0 .. 255.
All inputs are finite; a program needn't handle non-finite values.
Results may differ from the reference program's by a relative error of at most 0.0029.
Values may be sent and summed in bfloat16 or wider, within the bound.
No kernel may reach another device: no remote copies, remote signals or barrier semaphores. Data moves between devices by JAX's collectives and lax.ppermute only.
A program may use at most 64 MiB of HBM per device.

```python
import math
import jax
import jax.numpy as jnp
from jax import lax

F = 4096
TR_DEV = 256
QB = 256
STEPS = 3
LAYERS = 4
NTRAIN = 1024
NQ = 1024
N_BLK = 4


def shard_levels(rng, dims, pieces, low, high):
    loudness, own = 1.0, jax.random.fold_in(rng, 6)
    for position, blocks in pieces:
        steps = jnp.exp(jax.random.uniform(jax.random.fold_in(own, position), (blocks,), jnp.float32, low / len(pieces), high / len(pieces)))
        loudness = loudness * jnp.repeat(steps, dims[position] // blocks).reshape([-1 if axis == position else 1 for axis in range(len(dims))])
    return loudness


def gaussian(own_key, dims, scale, limit, cuts=(), kind=jnp.bfloat16):
    loudness = shard_levels(own_key, dims, cuts, -0.22, 0.18) if cuts else 1.0
    drawn = jax.random.normal(own_key, dims, jnp.float32) * scale * loudness
    return jnp.minimum(jnp.maximum(drawn, -limit), limit).astype(kind)


def setup_inputs(seed: int = 0, part: int = 0) -> dict:
    keys = jax.random.split(jax.random.key(seed), 5)
    own_keys = jax.random.split(jax.random.fold_in(keys[4], part), 5)
    return {
        "train_grads": gaussian(own_keys[0], (NTRAIN, LAYERS, F), 1.0, 6.0, ((0, 4), (1, 4))),
        "query_grads": gaussian(own_keys[1], (NQ, LAYERS, F), 1.0, 6.0, ((0, 4), (1, 4))),
        "eigenvalues": jnp.clip(jnp.exp(math.log(2.0) - 4.6051702 * jax.random.uniform(keys[2], (LAYERS, F), jnp.float32) ** shard_levels(keys[2], (LAYERS, F), ((0, 4),), -0.2, 0.2)), 0.02, 2.0),
        "order": jax.vmap(lambda own: jax.random.permutation(own, QB))(jax.random.split(own_keys[3], STEPS)).reshape((STEPS, QB)).astype(jnp.int32),
    }


def reference(train_grads, query_grads, eigenvalues, order):
    weights = 1.0 / (eigenvalues + 0.05)
    scaled = (query_grads.astype(jnp.float32) * weights[None, :, :]).astype(jnp.bfloat16)
    tf = train_grads.astype(jnp.float32)
    selfinf = lax.optimization_barrier(jnp.sum(tf * tf * weights[None, :, :], axis=(1, 2)))
    inverse = 1.0 / jnp.sqrt(selfinf)
    q_blocks = scaled.reshape(N_BLK, QB, LAYERS * F)
    t_blocks = train_grads.reshape(N_BLK, TR_DEV, LAYERS * F)
    slabs = jnp.arange(N_BLK, dtype=jnp.int32)
    results = []
    for step in range(STEPS):

        def one_slab(slab):
            source = (slab - step) % N_BLK
            return lax.dot_general(q_blocks[source], t_blocks[slab], (((1,), (1,)), ((), ())), preferred_element_type=jnp.float32)
        raw = lax.map(one_slab, slabs)
        raw = jnp.transpose(raw, (1, 0, 2)).reshape(QB, NTRAIN)
        raw = jnp.take(raw, order[step], axis=0)
        results.append(raw * inverse[None, :])
    return jnp.stack(results, axis=0)
```

```python
import functools

import jax
import jax.numpy as jnp
from jax import lax
from jax.experimental import pallas as pl
from jax.experimental.pallas import tpu as pltpu
from jax.sharding import PartitionSpec as P

STEPS = 3
TAIL = 64
DEPTH = 512
EXTRA = 8
F32, BF16 = jnp.float32, jnp.bfloat16


def after(x, *earlier):
    return lax.optimization_barrier((x,) + earlier)[0]


def scaled(x, weights):
    return (x.astype(F32) * weights).astype(BF16)


def dot_rows(x, t):
    return lax.dot_general(x, t, (((1,), (1,)), ((), ())), preferred_element_type=F32)


def choose(order_row, p):
    queries = p.shape[0]
    hot = (lax.broadcasted_iota(jnp.int32, (queries, order_row.shape[1]), 0) == order_row).astype(F32).astype(BF16)
    total = None
    for _ in range(3):
        term = p.astype(BF16)
        p = p - term.astype(F32)
        part = lax.dot_general(hot, term, (((0,), (0,)), ((), ())), preferred_element_type=F32)
        total = part if total is None else total + part
    return total


def block_kernel(kind, layers, *refs):
    place, x_refs = refs[0], refs[1 : 1 + (2 if kind == "mixed" else 1)]
    refs = refs[1 + len(x_refs) :]
    t_ref, eig_ref, order_ref = refs[:3]
    outs, (acc, self_acc) = refs[3 : 3 + layers], refs[3 + layers :]
    step, steps = pl.program_id(0), pl.num_programs(0)
    me, odd = place[0], place[1]

    @pl.when(step == 0)
    def _():
        acc[...] = jnp.zeros_like(acc)
        self_acc[...] = jnp.zeros_like(self_acc)

    weights = 1.0 / (eig_ref[...] + 0.05)
    t = t_ref[...]
    if kind == "mixed":

        @pl.when(odd == 1)
        def _():
            acc[...] += dot_rows(scaled(x_refs[0][...], weights), t)

        @pl.when(odd == 0)
        def _():
            head = x_refs[1].shape[0]
            acc[:head] += dot_rows(scaled(x_refs[1][...], weights), t)

    else:
        acc[...] += dot_rows(scaled(x_refs[0][...], weights), t)
    if kind == "first":
        tf = t.astype(F32)
        square = tf * tf * weights
        part = square[:, :128]
        for k in range(128, square.shape[1], 128):
            part = part + square[:, k : k + 128]
        self_acc[...] += part

    @pl.when(step == steps - 1)
    def _():
        acc[...] = choose(order_ref[...], acc[...])
        own = acc.shape[0] // layers
        if kind == "first":
            row = jnp.sum(self_acc[...].T, axis=0, keepdims=True)
            extra = jnp.broadcast_to(row, (EXTRA, row.shape[1]))
        for by in range(layers):
            start = pl.multiple_of(lax.rem(me + by, layers) * own, own)
            outs[by][:own] = acc[pl.ds(start, own)]
            if kind == "first":
                outs[by][own:] = extra


def block_call(kind, layers, place, xs, t, eig, order_row):
    rows, depth = t.shape
    queries = order_row.shape[1]
    own = queries // layers + (EXTRA if kind == "first" else 0)
    x_specs = [pl.BlockSpec((x.shape[0], DEPTH), lambda k, place: (0, k)) for x in xs]
    if kind == "mixed":
        x_specs[0] = pl.BlockSpec((queries, DEPTH), lambda k, place: (0, k * place[1]))
        x_specs[1] = pl.BlockSpec((xs[1].shape[0], DEPTH), lambda k, place: (0, k * (1 - place[1])))
    return pl.pallas_call(
        functools.partial(block_kernel, kind, layers),
        grid_spec=pltpu.PrefetchScalarGridSpec(
            num_scalar_prefetch=1,
            grid=(depth // DEPTH,),
            in_specs=x_specs
            + [
                pl.BlockSpec((rows, DEPTH), lambda k, place: (0, k)),
                pl.BlockSpec((1, DEPTH), lambda k, place: (0, k)),
                pl.BlockSpec((1, queries), lambda k, place: (0, 0)),
            ],
            out_specs=[pl.BlockSpec((own, rows), lambda k, place: (0, 0))] * layers,
            scratch_shapes=[pltpu.VMEM((queries, rows), F32), pltpu.VMEM((rows, 128), F32)],
        ),
        out_shape=[jax.ShapeDtypeStruct((own, rows), F32)] * layers,
        compiler_params=pltpu.CompilerParams(vmem_limit_bytes=24 << 20),
        cost_estimate=pl.CostEstimate(
            flops=2 * queries * rows * depth, bytes_accessed=4 * queries * depth, transcendentals=0
        ),
        name="block_" + kind,
    )(place, *xs, t, eig, order_row)


def tail_kernel(x_ref, t_ref, eig_ref, out_ref):
    @pl.when(pl.program_id(0) == 0)
    def _():
        out_ref[...] = jnp.zeros_like(out_ref)

    out_ref[...] += dot_rows(scaled(x_ref[...], 1.0 / (eig_ref[...] + 0.05)), t_ref[...])


def tail_call(x, t, eig):
    rows, depth = t.shape
    tail = x.shape[0]
    return pl.pallas_call(
        tail_kernel,
        grid=(depth // DEPTH,),
        in_specs=[
            pl.BlockSpec((tail, DEPTH), lambda k: (0, k)),
            pl.BlockSpec((rows, DEPTH), lambda k: (0, k)),
            pl.BlockSpec((1, DEPTH), lambda k: (0, k)),
        ],
        out_specs=pl.BlockSpec((tail, rows), lambda k: (0, 0)),
        out_shape=jax.ShapeDtypeStruct((tail, rows), F32),
        compiler_params=pltpu.CompilerParams(vmem_limit_bytes=24 << 20),
        cost_estimate=pl.CostEstimate(flops=2 * tail * rows * depth, bytes_accessed=2 * rows * depth, transcendentals=0),
        name="tail_product",
    )(x, t, eig)


def added(refs):
    total = refs[0][...]
    for ref in refs[1:]:
        total = total + ref[...]
    return total


def base_kernel(layers, *refs):
    ins, (out_ref, inverse_ref) = refs[:-2], refs[-2:]
    own = out_ref.shape[1]
    first, second = added(ins[:layers]), added(ins[layers:])
    inverse = 1.0 / jnp.sqrt(first[own : own + 1])
    inverse_ref[...] = inverse
    out_ref[0] = first[:own] * inverse
    out_ref[1] = second * inverse
    out_ref[2] = jnp.zeros_like(second)


def base_call(layers, sums0, sums1):
    own, rows = sums1[0].shape
    return pl.pallas_call(
        functools.partial(base_kernel, layers),
        out_shape=[jax.ShapeDtypeStruct((STEPS, own, rows), F32), jax.ShapeDtypeStruct((1, rows), F32)],
        name="base",
    )(*sums0, *sums1)


def final_kernel(layers, first_row, base_ref, inverse_ref, order_ref, *refs):
    sums, terms, out_ref = refs[:layers], refs[layers:-1], refs[-1]
    chosen = choose(order_ref[...] - first_row, added(terms))
    out_ref[0] = (added(sums) + chosen) * inverse_ref[...]


def final_call(layers, first_row, base, inverse, order_row, sums, terms):
    _, own, rows = base.shape
    last = pl.BlockSpec((1, own, rows), lambda i: (STEPS - 1, 0, 0))

    def whole(x):
        return pl.BlockSpec(x.shape, lambda i: (0, 0))

    return pl.pallas_call(
        functools.partial(final_kernel, layers, first_row),
        grid=(1,),
        in_specs=[pl.BlockSpec(memory_space=pl.ANY), whole(inverse), whole(order_row)]
        + [whole(x) for x in (*sums, *terms)],
        out_specs=last,
        out_shape=jax.ShapeDtypeStruct(base.shape, F32),
        input_output_aliases={0: 0},
        name="final",
    )(base, inverse, order_row, *sums, *terms)


def per_device(train_grads, query_grads, eigenvalues, order):
    rows, queries = train_grads.shape[0], query_grads.shape[0]
    blks, layers = lax.axis_size("blk"), lax.axis_size("layer")
    own = queries // layers
    head = queries - TAIL
    me = lax.axis_index("layer")
    place = jnp.stack([me, lax.axis_index("blk") % 2]).astype(jnp.int32)
    evens = range(0, blks, 2)
    t = train_grads.reshape(rows, -1)
    q = query_grads.reshape(queries, -1)
    order_rows = [order[s : s + 1] for s in range(STEPS)]
    own_order = lax.dynamic_slice(order_rows[2], (0, me * own), (1, own))

    odd_on = [(i + 1, (i + 3) % blks) for i in evens]
    even_on = [(i, (i + 2) % blks) for i in evens]
    to_odd = [(i, i + 1) for i in evens]
    to_even = [(i + 1, i) for i in evens]

    def exchange(pieces):
        got = [pieces[0]]
        for by in range(1, layers):
            got.append(lax.ppermute(pieces[by], "layer", [(i, (i + by) % layers) for i in range(layers)]))
        return got

    odd_two = lax.ppermute(q, "blk", odd_on)
    odd_one = lax.ppermute(q, "blk", to_odd)
    sums0 = exchange(block_call("first", layers, place, [q], t, eigenvalues, order_rows[0]))
    main, last = lax.optimization_barrier((q[:head], q[head:], *sums0))[:2]
    even_one = lax.ppermute(after(odd_two, main, last), "blk", to_even)
    main = lax.ppermute(main, "blk", even_on)
    last = lax.ppermute(last, "blk", even_on)

    sums1 = exchange(block_call("mixed", layers, place, [odd_one, even_one], t, eigenvalues, order_rows[1]))
    base, inverse = base_call(layers, sums0, sums1)

    main = after(main, inverse)
    pieces2 = block_call("mixed", layers, place, [odd_two, main], t, eigenvalues, order_rows[2])
    sums2 = exchange(pieces2)
    tail = tail_call(after(last, *pieces2), t, eigenvalues)
    terms = [tail]
    for by in range(1, layers):
        pairs = [(i * layers + k, i * layers + (k + by) % layers) for i in evens for k in range(layers)]
        terms.append(lax.ppermute(tail, ("blk", "layer"), pairs))
    return final_call(layers, head, base, inverse, own_order, sums2, terms)


def solution(mesh):
    return jax.shard_map(
        per_device,
        mesh=mesh,
        in_specs=(
            P(("groups", "blk"), "layer", None),
            P(("groups", "blk"), "layer", None),
            P("layer", None),
            P("groups", None),
        ),
        out_specs=P(None, "layer", ("groups", "blk")),
        check_vma=False,
    )
```

```python
import functools

import jax
import jax.numpy as jnp
from jax import lax
from jax.experimental import pallas as pl
from jax.experimental.pallas import tpu as pltpu
from jax.sharding import PartitionSpec as P

STEPS = 3
PART = 1024
EXTRA = 8
F32, BF16 = jnp.float32, jnp.bfloat16
VMEM = pl.BlockSpec(memory_space=pltpu.VMEM)
SMEM = pl.BlockSpec(memory_space=pltpu.SMEM)


def after(x, *earlier):
    return lax.optimization_barrier((x,) + earlier)[0]


def dot(x, y, contract):
    return lax.dot_general(x, y, (contract, ((), ())), preferred_element_type=F32)


def added(refs):
    total = refs[0][...].astype(F32)
    for ref in refs[1:]:
        total = total + ref[...].astype(F32)
    return total


def choose(column, p):
    shape = (column.shape[0], p.shape[0])
    hot = (lax.broadcasted_iota(jnp.int32, shape, 1) == column).astype(F32).astype(BF16)
    total = None
    for _ in range(3):
        term = p.astype(BF16)
        p = p - term.astype(F32)
        part = dot(hot, term, ((1,), (0,)))
        total = part if total is None else total + part
    return total


def scores_kernel(step, first, layers, me_ref, x_ref, t_ref, eig_ref, order_ref, *refs):
    outs, acc = refs[:layers], refs[layers]
    p, squares = None, None
    for c in range(0, t_ref.shape[1], PART):
        columns = slice(c, c + PART)
        weights = 1.0 / (eig_ref[:, columns] + 0.05)
        t = t_ref[:, columns]
        x = (x_ref[:, columns].astype(F32) * weights).astype(BF16)
        part = dot(x, t, ((1,), (1,)))
        p = part if p is None else p + part
        if first:
            tf = t.astype(F32)
            square = tf * tf * weights
            for k in range(0, PART, 128):
                part = square[:, k : k + 128]
                squares = part if squares is None else squares + part
    acc[...] = choose(order_ref[:, step : step + 1], p)
    own = p.shape[0] // layers
    if first:
        extra = jnp.broadcast_to(jnp.sum(squares.T, axis=0, keepdims=True), (EXTRA, p.shape[1]))
    for by in range(layers):
        start = pl.multiple_of(lax.rem(me_ref[0] + by, layers) * own, own)
        outs[by][:own] = acc[pl.ds(start, own)].astype(outs[by].dtype)
        if first:
            outs[by][own:] = extra


def scores_call(step, first, layers, me, x, t, eig, order, sent):
    rows, depth = t.shape
    queries = x.shape[0]
    own = queries // layers + (EXTRA if first else 0)
    return pl.pallas_call(
        functools.partial(scores_kernel, step, first, layers),
        in_specs=[SMEM] + [VMEM] * 4,
        out_specs=[VMEM] * layers,
        scratch_shapes=[pltpu.VMEM((queries, rows), F32)],
        out_shape=[jax.ShapeDtypeStruct((own, rows), F32 if by == 0 else sent) for by in range(layers)],
        compiler_params=pltpu.CompilerParams(vmem_limit_bytes=24 << 20),
        cost_estimate=pl.CostEstimate(
            flops=2 * queries * rows * depth, bytes_accessed=4 * queries * depth, transcendentals=0
        ),
        name="scores_step_" + str(step),
    )(me, x, t, eig, order)


def base_kernel(layers, *refs):
    ins, (out_ref, inverse_ref) = refs[:-2], refs[-2:]
    own = out_ref.shape[1]
    first, second = added(ins[:layers]), added(ins[layers:])
    inverse = 1.0 / jnp.sqrt(first[own : own + 1])
    inverse_ref[...] = inverse
    out_ref[0] = first[:own] * inverse
    out_ref[1] = second * inverse
    out_ref[2] = jnp.zeros_like(second)


def base_call(layers, sums0, sums1):
    own, rows = sums1[0].shape
    return pl.pallas_call(
        functools.partial(base_kernel, layers),
        out_shape=[jax.ShapeDtypeStruct((STEPS, own, rows), F32), jax.ShapeDtypeStruct((1, rows), F32)],
        name="base",
    )(*sums0, *sums1)


def final_kernel(base_ref, inverse_ref, *refs):
    refs[-1][0] = added(refs[:-1]) * inverse_ref[...]


def final_call(base, inverse, sums):
    _, own, rows = base.shape
    whole = lambda i: (0, 0)
    return pl.pallas_call(
        final_kernel,
        grid=(1,),
        in_specs=[pl.BlockSpec(memory_space=pl.ANY)] + [pl.BlockSpec(x.shape, whole) for x in (inverse, *sums)],
        out_specs=pl.BlockSpec((1, own, rows), lambda i: (STEPS - 1, 0, 0)),
        out_shape=jax.ShapeDtypeStruct(base.shape, F32),
        input_output_aliases={0: 0},
        name="final",
    )(base, inverse, *sums)


def per_device(train_grads, query_grads, eigenvalues, order):
    rows, queries = train_grads.shape[0], query_grads.shape[0]
    layers = lax.axis_size("layer")
    me = lax.axis_index("layer").astype(jnp.int32).reshape(1)
    t = train_grads.reshape(rows, -1)
    q = query_grads.reshape(queries, -1)
    columns = order.T

    def shifted(x, axis, by):
        length = lax.axis_size(axis)
        return lax.ppermute(x, axis, [(i, (i + by) % length) for i in range(length)])

    def exchange(pieces):
        return [pieces[0]] + [shifted(pieces[by], "layer", by) for by in range(1, layers)]

    one_back = shifted(q, "blk", 1)
    sums0 = exchange(scores_call(0, True, layers, me, q, t, eigenvalues, columns, F32))
    one_back = after(one_back, *sums0)
    two_back = shifted(one_back, "blk", 1)
    sums1 = exchange(scores_call(1, False, layers, me, one_back, t, eigenvalues, columns, F32))
    base, inverse = base_call(layers, sums0, sums1)
    t2 = after(t, inverse)
    sums2 = exchange(scores_call(2, False, layers, me, two_back, t2, eigenvalues, columns, BF16))
    return final_call(base, inverse, sums2)


def solution(mesh):
    return jax.shard_map(
        per_device,
        mesh=mesh,
        in_specs=(
            P(("groups", "blk"), "layer", None),
            P(("groups", "blk"), "layer", None),
            P("layer", None),
            P("groups", None),
        ),
        out_specs=P(None, "layer", ("groups", "blk")),
        check_vma=False,
    )
```

```python
import functools

import jax
import jax.numpy as jnp
from jax import lax
from jax.experimental import pallas as pl
from jax.experimental.pallas import tpu as pltpu
from jax.sharding import PartitionSpec as P

STEPS = 3
PART = 1024
EXTRA = 8
F32, BF16 = jnp.float32, jnp.bfloat16
VMEM = pl.BlockSpec(memory_space=pltpu.VMEM)
SMEM = pl.BlockSpec(memory_space=pltpu.SMEM)


def after(x, *earlier):
    return lax.optimization_barrier((x,) + earlier)[0]


def dot(x, y, contract):
    return lax.dot_general(x, y, (contract, ((), ())), preferred_element_type=F32)


def added(refs):
    total = refs[0][...].astype(F32)
    for ref in refs[1:]:
        total = total + ref[...].astype(F32)
    return total


def choose(column, p):
    shape = (column.shape[0], p.shape[0])
    hot = (lax.broadcasted_iota(jnp.int32, shape, 1) == column).astype(F32).astype(BF16)
    total = None
    for _ in range(3):
        term = p.astype(BF16)
        p = p - term.astype(F32)
        part = dot(hot, term, ((1,), (0,)))
        total = part if total is None else total + part
    return total


def scores_kernel(step, first, layers, me_ref, x_ref, t_ref, eig_ref, order_ref, *refs):
    outs, acc = refs[:layers], refs[layers]
    p, squares = None, None
    for c in range(0, t_ref.shape[1], PART):
        columns = slice(c, c + PART)
        weights = 1.0 / (eig_ref[:, columns] + 0.05)
        t = t_ref[:, columns]
        x = (x_ref[:, columns].astype(F32) * weights).astype(BF16)
        part = dot(x, t, ((1,), (1,)))
        p = part if p is None else p + part
        if first:
            tf = t.astype(F32)
            square = tf * tf * weights
            for k in range(0, PART, 128):
                part = square[:, k : k + 128]
                squares = part if squares is None else squares + part
    acc[...] = choose(order_ref[:, step : step + 1], p)
    own = p.shape[0] // layers
    if first:
        extra = jnp.broadcast_to(jnp.sum(squares.T, axis=0, keepdims=True), (EXTRA, p.shape[1]))
    for by in range(layers):
        start = pl.multiple_of(lax.rem(me_ref[0] + by, layers) * own, own)
        outs[by][:own] = acc[pl.ds(start, own)].astype(outs[by].dtype)
        if first:
            outs[by][own:] = extra


def scores_call(step, first, layers, me, x, t, eig, order, sent):
    rows, depth = t.shape
    queries = x.shape[0]
    own = queries // layers + (EXTRA if first else 0)
    return pl.pallas_call(
        functools.partial(scores_kernel, step, first, layers),
        in_specs=[SMEM] + [VMEM] * 4,
        out_specs=[VMEM] * layers,
        scratch_shapes=[pltpu.VMEM((queries, rows), F32)],
        out_shape=[jax.ShapeDtypeStruct((own, rows), F32 if by == 0 else sent) for by in range(layers)],
        compiler_params=pltpu.CompilerParams(vmem_limit_bytes=12 << 20),
        cost_estimate=pl.CostEstimate(
            flops=2 * queries * rows * depth, bytes_accessed=4 * queries * depth, transcendentals=0
        ),
        name="scores_step_" + str(step),
    )(me, x, t, eig, order)


def base_kernel(layers, *refs):
    ins, (out_ref, inverse_ref) = refs[:-2], refs[-2:]
    own = out_ref.shape[1]
    first, second = added(ins[:layers]), added(ins[layers:])
    inverse = 1.0 / jnp.sqrt(first[own : own + 1])
    inverse_ref[...] = inverse
    out_ref[0] = first[:own] * inverse
    out_ref[1] = second * inverse
    out_ref[2] = jnp.zeros_like(second)


def base_call(layers, sums0, sums1):
    own, rows = sums1[0].shape
    return pl.pallas_call(
        functools.partial(base_kernel, layers),
        out_shape=[jax.ShapeDtypeStruct((STEPS, own, rows), F32), jax.ShapeDtypeStruct((1, rows), F32)],
        compiler_params=pltpu.CompilerParams(vmem_limit_bytes=4 << 20),
        name="base",
    )(*sums0, *sums1)


def per_device(train_grads, query_grads, eigenvalues, order):
    rows, queries = train_grads.shape[0], query_grads.shape[0]
    layers = lax.axis_size("layer")
    me = lax.axis_index("layer").astype(jnp.int32).reshape(1)
    t = train_grads.reshape(rows, -1)
    q = query_grads.reshape(queries, -1)
    columns = order.T

    def shifted(x, axis, by):
        length = lax.axis_size(axis)
        return lax.ppermute(x, axis, [(i, (i + by) % length) for i in range(length)])

    def exchange(pieces):
        return [pieces[0]] + [shifted(pieces[by], "layer", by) for by in range(1, layers)]

    one_back = shifted(q, "blk", 1)
    sums0 = exchange(scores_call(0, True, layers, me, q, t, eigenvalues, columns, F32))
    one_back = after(one_back, *sums0)
    two_back = shifted(one_back, "blk", 1)
    sums1 = exchange(scores_call(1, False, layers, me, one_back, t, eigenvalues, columns, F32))
    base, inverse = base_call(layers, sums0, sums1)
    t2 = after(t, inverse)
    sums2 = exchange(scores_call(2, False, layers, me, two_back, t2, eigenvalues, columns, BF16))
    total = sums2[0]
    for piece in sums2[1:]:
        total = total + piece.astype(F32)
    return lax.dynamic_update_slice(base, (total * inverse)[None], (STEPS - 1, 0, 0))


def solution(mesh):
    return jax.shard_map(
        per_device,
        mesh=mesh,
        in_specs=(
            P(("groups", "blk"), "layer", None),
            P(("groups", "blk"), "layer", None),
            P("layer", None),
            P("groups", None),
        ),
        out_specs=P(None, "layer", ("groups", "blk")),
        check_vma=False,
    )
```

```python
import functools

import jax
import jax.numpy as jnp
from jax import lax
from jax.experimental import pallas as pl
from jax.experimental.pallas import tpu as pltpu
from jax.sharding import PartitionSpec as P

STEPS = 3
PART = 1024
EXTRA = 8
F32, BF16 = jnp.float32, jnp.bfloat16
VMEM = pl.BlockSpec(memory_space=pltpu.VMEM)
SMEM = pl.BlockSpec(memory_space=pltpu.SMEM)


def after(x, *earlier):
    return lax.optimization_barrier((x,) + earlier)[0]


def dot(x, y, contract):
    return lax.dot_general(x, y, (contract, ((), ())), preferred_element_type=F32)


def added(refs):
    total = refs[0][...].astype(F32)
    for ref in refs[1:]:
        total = total + ref[...].astype(F32)
    return total


def choose(column, p):
    shape = (column.shape[0], p.shape[0])
    hot = (lax.broadcasted_iota(jnp.int32, shape, 1) == column).astype(F32).astype(BF16)
    total = None
    for _ in range(3):
        term = p.astype(BF16)
        p = p - term.astype(F32)
        part = dot(hot, term, ((1,), (0,)))
        total = part if total is None else total + part
    return total


def scores_kernel(step, first, layers, n_x, me_ref, *refs):
    x_refs, (t_ref, eig_ref, order_ref), refs = refs[:n_x], refs[n_x : n_x + 3], refs[n_x + 3 :]
    outs, acc = refs[:layers], refs[layers]
    p, squares = None, None
    for c in range(0, t_ref.shape[1], PART):
        columns = slice(c, c + PART)
        weights = 1.0 / (eig_ref[:, columns] + 0.05)
        t = t_ref[:, columns]
        x = x_refs[0][:, columns].astype(F32)
        for ref in x_refs[1:]:
            x = x + ref[:, columns].astype(F32)
        x = (x * weights).astype(BF16)
        part = dot(x, t, ((1,), (1,)))
        p = part if p is None else p + part
        if first:
            tf = t.astype(F32)
            square = tf * tf * weights
            for k in range(0, PART, 128):
                part = square[:, k : k + 128]
                squares = part if squares is None else squares + part
    acc[...] = choose(order_ref[:, step : step + 1], p)
    own = p.shape[0] // layers
    if first:
        extra = jnp.broadcast_to(jnp.sum(squares.T, axis=0, keepdims=True), (EXTRA, p.shape[1]))
    for by in range(layers):
        start = pl.multiple_of((me_ref[0] ^ by) * own, own)
        outs[by][:own] = acc[pl.ds(start, own)].astype(outs[by].dtype)
        if first:
            outs[by][own:] = extra


def scores_call(step, first, layers, me, xs, t, eig, order, sent):
    rows, depth = t.shape
    queries = xs[0].shape[0]
    own = queries // layers + (EXTRA if first else 0)
    return pl.pallas_call(
        functools.partial(scores_kernel, step, first, layers, len(xs)),
        in_specs=[SMEM] + [VMEM] * (len(xs) + 3),
        out_specs=[VMEM] * layers,
        scratch_shapes=[pltpu.VMEM((queries, rows), F32)],
        out_shape=[jax.ShapeDtypeStruct((own, rows), F32 if by == 0 else sent) for by in range(layers)],
        compiler_params=pltpu.CompilerParams(vmem_limit_bytes=12 << 20),
        cost_estimate=pl.CostEstimate(
            flops=2 * queries * rows * depth, bytes_accessed=4 * queries * depth, transcendentals=0
        ),
        name="scores_step_" + str(step),
    )(me, *xs, t, eig, order)


def base_kernel(layers, *refs):
    ins, (out_ref, inverse_ref) = refs[:-2], refs[-2:]
    own = out_ref.shape[1]
    first, second = added(ins[:layers]), added(ins[layers:])
    inverse = 1.0 / jnp.sqrt(first[own : own + 1])
    inverse_ref[...] = inverse
    out_ref[0] = first[:own] * inverse
    out_ref[1] = second * inverse
    out_ref[2] = jnp.zeros_like(second)


def base_call(layers, sums0, sums1):
    own, rows = sums1[0].shape
    return pl.pallas_call(
        functools.partial(base_kernel, layers),
        out_shape=[jax.ShapeDtypeStruct((STEPS, own, rows), F32), jax.ShapeDtypeStruct((1, rows), F32)],
        compiler_params=pltpu.CompilerParams(vmem_limit_bytes=4 << 20),
        name="base",
    )(*sums0, *sums1)


def per_device(train_grads, query_grads, eigenvalues, order):
    rows, queries = train_grads.shape[0], query_grads.shape[0]
    layers, blks = lax.axis_size("layer"), lax.axis_size("blk")
    me = lax.axis_index("layer").astype(jnp.int32).reshape(1)
    t = train_grads.reshape(rows, -1)
    q = query_grads.reshape(queries, -1)
    columns = order.T

    def exchange(pieces):
        order = [1, *range(layers - 1, 1, -1)]
        got = [lax.ppermute(pieces[by], "layer", [(i, i ^ by) for i in range(layers)]) for by in order]
        return [pieces[0]] + got

    one_back = lax.ppermute(q, "blk", [(i, (i + 1) % blks) for i in range(blks)])
    sums0 = exchange(scores_call(0, True, layers, me, [q], t, eigenvalues, columns, F32))
    later = after(q, *sums0)
    even_two = lax.ppermute(later, "blk", [(i, (i + 2) % blks) for i in range(0, blks, 2)])
    one_back = after(one_back, later)
    odd_two = lax.ppermute(one_back, "blk", [(i, i + 1) for i in range(0, blks, 2)])
    sums1 = exchange(scores_call(1, False, layers, me, [one_back], t, eigenvalues, columns, F32))
    base, inverse = base_call(layers, sums0, sums1)
    t2 = after(t, inverse)
    sums2 = exchange(scores_call(2, False, layers, me, [even_two, odd_two], t2, eigenvalues, columns, BF16))
    total = sums2[0]
    for piece in sums2[1:]:
        total = total + piece.astype(F32)
    return lax.dynamic_update_slice(base, (total * inverse)[None], (STEPS - 1, 0, 0))


def solution(mesh):
    return jax.shard_map(
        per_device,
        mesh=mesh,
        in_specs=(
            P(("groups", "blk"), "layer", None),
            P(("groups", "blk"), "layer", None),
            P("layer", None),
            P("groups", None),
        ),
        out_specs=P(None, "layer", ("groups", "blk")),
        check_vma=False,
    )
```

```python
import functools

import jax
import jax.numpy as jnp
from jax import lax
from jax.experimental import pallas as pl
from jax.experimental.pallas import tpu as pltpu
from jax.sharding import PartitionSpec as P

STEPS = 3
PART = 1024
EXTRA = 8
F32, BF16 = jnp.float32, jnp.bfloat16
VMEM = pl.BlockSpec(memory_space=pltpu.VMEM)
SMEM = pl.BlockSpec(memory_space=pltpu.SMEM)


def after(x, *earlier):
    return lax.optimization_barrier((x,) + earlier)[0]


def dot(x, y, contract):
    return lax.dot_general(x, y, (contract, ((), ())), preferred_element_type=F32)


def added(refs):
    total = refs[0][...].astype(F32)
    for ref in refs[1:]:
        total = total + ref[...].astype(F32)
    return total


def choose(column, p):
    hot = one_hot(column, p.shape[0])
    total = None
    for _ in range(3):
        term = p.astype(BF16)
        p = p - term.astype(F32)
        part = dot(hot, term, ((1,), (0,)))
        total = part if total is None else total + part
    return total


def weights_of(eig_ref, columns):
    return 1.0 / (eig_ref[:, columns] + 0.05)


def one_hot(column, length):
    shape = (column.shape[0], length)
    return (lax.broadcasted_iota(jnp.int32, shape, 1) == column).astype(F32).astype(BF16)


def scores_kernel(steps, first, layers, me_ref, *refs):
    x_refs, refs = [], refs
    for _, n in steps:
        x_refs.append(refs[:n])
        refs = refs[n:]
    (t_ref, eig_ref, order_ref), refs = refs[:3], refs[3:]
    outs, acc = refs[:layers], refs[layers]
    p, squares = [None] * len(steps), None
    for c in range(0, t_ref.shape[1], PART):
        columns = slice(c, c + PART)
        weights = weights_of(eig_ref, columns)
        t = t_ref[:, columns]
        for i, group in enumerate(x_refs):
            x = (added([ref.at[:, columns] for ref in group]) * weights).astype(BF16)
            part = dot(x, t, ((1,), (1,)))
            p[i] = part if p[i] is None else p[i] + part
        if first:
            tf = t.astype(F32)
            square = tf * tf * weights
            for k in range(0, PART, 128):
                part = square[:, k : k + 128]
                squares = part if squares is None else squares + part
    own = acc.shape[0] // layers
    for i, (step, _) in enumerate(steps):
        acc[...] = choose(order_ref[:, step : step + 1], p[i])
        for by in range(layers):
            start = pl.multiple_of((me_ref[0] ^ by) * own, own)
            outs[by][i * own : (i + 1) * own] = acc[pl.ds(start, own)].astype(outs[by].dtype)
    if first:
        extra = jnp.broadcast_to(jnp.sum(squares.T, axis=0, keepdims=True), (EXTRA, acc.shape[1]))
        for by in range(layers):
            outs[by][len(steps) * own :] = extra


def scores_call(steps, first, layers, me, xs, t, eig, order, sent):
    rows, depth = t.shape
    queries = xs[0].shape[0]
    share = len(steps) * (queries // layers) + (EXTRA if first else 0)
    return pl.pallas_call(
        functools.partial(scores_kernel, steps, first, layers),
        in_specs=[SMEM] + [VMEM] * (len(xs) + 3),
        out_specs=[VMEM] * layers,
        scratch_shapes=[pltpu.VMEM((queries, rows), F32)],
        out_shape=[jax.ShapeDtypeStruct((share, rows), F32 if by == 0 else sent) for by in range(layers)],
        compiler_params=pltpu.CompilerParams(vmem_limit_bytes=12 << 20),
        cost_estimate=pl.CostEstimate(
            flops=2 * len(steps) * queries * rows * depth, bytes_accessed=4 * queries * depth, transcendentals=0
        ),
        name="scores_" + "_".join(str(step) for step, _ in steps),
    )(me, *xs, t, eig, order)


def ordered_kernel(step, layers, me_ref, q_ref, eig_ref, order_ref, *refs):
    outs, hot = refs[:layers], refs[layers]
    queries = q_ref.shape[0]
    own = queries // layers
    for by in range(layers):
        start = pl.multiple_of((me_ref[0] ^ by) * own, own)
        hot[by * own : (by + 1) * own] = one_hot(order_ref[pl.ds(start, own), step : step + 1], queries)
    for c in range(0, q_ref.shape[1], PART):
        columns = slice(c, c + PART)
        x = (q_ref[:, columns].astype(F32) * weights_of(eig_ref, columns)).astype(BF16)
        x = dot(hot[...], x, ((1,), (0,))).astype(BF16)
        for by in range(layers):
            outs[by][:, columns] = x[by * own : (by + 1) * own]


def ordered_call(step, layers, me, q, eig, order):
    queries, depth = q.shape
    return pl.pallas_call(
        functools.partial(ordered_kernel, step, layers),
        in_specs=[SMEM] + [VMEM] * 3,
        out_specs=[VMEM] * layers,
        scratch_shapes=[pltpu.VMEM((queries, queries), BF16)],
        out_shape=[jax.ShapeDtypeStruct((queries // layers, depth), BF16)] * layers,
        compiler_params=pltpu.CompilerParams(vmem_limit_bytes=16 << 20),
        cost_estimate=pl.CostEstimate(
            flops=2 * queries * queries * depth, bytes_accessed=4 * queries * depth, transcendentals=0
        ),
        name="ordered",
    )(me, q, eig, order)


def product_kernel(x_ref, t_ref, out_ref):
    out_ref[...] = dot(x_ref[...], t_ref[...], ((1,), (1,))).astype(out_ref.dtype)


def product_call(x, t, dtype):
    (own, depth), rows = x.shape, t.shape[0]
    return pl.pallas_call(
        product_kernel,
        in_specs=[VMEM] * 2,
        out_specs=VMEM,
        out_shape=jax.ShapeDtypeStruct((own, rows), dtype),
        compiler_params=pltpu.CompilerParams(vmem_limit_bytes=8 << 20),
        cost_estimate=pl.CostEstimate(flops=2 * own * rows * depth, bytes_accessed=2 * rows * depth, transcendentals=0),
        name="product",
    )(x, t)


def base_kernel(layers, *refs):
    ins, (out_ref, rest_ref, inverse_ref) = refs[:-3], refs[-3:]
    own = out_ref.shape[1]
    first, second = added(ins[:layers]), added(ins[layers:])
    inverse = 1.0 / jnp.sqrt(first[own : own + 1])
    inverse_ref[...] = inverse
    out_ref[0] = first[:own] * inverse
    out_ref[1] = second[:own] * inverse
    out_ref[2] = jnp.zeros_like(out_ref[2])
    rest_ref[...] = second[own:]


def base_call(layers, own, sums0, sums1):
    rows = sums1[0].shape[1]
    return pl.pallas_call(
        functools.partial(base_kernel, layers),
        out_shape=[
            jax.ShapeDtypeStruct((STEPS, own, rows), F32),
            jax.ShapeDtypeStruct((own, rows), F32),
            jax.ShapeDtypeStruct((1, rows), F32),
        ],
        compiler_params=pltpu.CompilerParams(vmem_limit_bytes=4 << 20),
        name="base",
    )(*sums0, *sums1)


def per_device(train_grads, query_grads, eigenvalues, order):
    rows, queries = train_grads.shape[0], query_grads.shape[0]
    layers, blks = lax.axis_size("layer"), lax.axis_size("blk")
    me = lax.axis_index("layer").astype(jnp.int32).reshape(1)
    t = train_grads.reshape(rows, -1)
    q = query_grads.reshape(queries, -1)
    columns = order.T
    evens = range(0, blks, 2)
    even_on = [(i, (i + 2) % blks) for i in evens]

    def exchange(pieces):
        bys = [1, *range(layers - 1, 1, -1)]
        got = [lax.ppermute(pieces[by], "layer", [(i, i ^ by) for i in range(layers)]) for by in bys]
        return [pieces[0]] + got

    odd_two = lax.ppermute(q, "blk", [(i + 1, (i + 3) % blks) for i in evens])
    odd_one = lax.ppermute(q, "blk", [(i, i + 1) for i in evens])
    pieces = scores_call(((0, 1),), True, layers, me, [q], t, eigenvalues, columns, F32)
    sums0 = exchange(pieces)

    ordered = ordered_call(2, layers, me, after(q, *pieces), eigenvalues, columns)
    bys = [*range(layers - 1, 0, -1), 0]
    parts = [ordered[by] for by in bys]
    parts[0], parts[1] = lax.optimization_barrier((parts[0], parts[1], *sums0))[:2]
    odd_two = after(odd_two, parts[0], parts[1])
    parts[2] = after(parts[2], odd_two)

    even_one = lax.ppermute(odd_two, "blk", [(i + 1, i) for i in evens])
    xs = [odd_one, even_one, odd_two]
    pieces = scores_call(((1, 2), (2, 1)), False, layers, me, xs, t, eigenvalues, columns, BF16)
    parts[3:] = lax.optimization_barrier((*parts[3:], *pieces))[: layers - 3]
    sums1 = exchange(pieces)
    base, total, inverse = base_call(layers, queries // layers, sums0, sums1)

    got = [lax.ppermute(part, "blk", even_on) for part in parts]
    for by, part in zip(bys[:-1], got):
        mine = product_call(part, t, BF16)
        total = total + lax.ppermute(mine, "layer", [(i, i ^ by) for i in range(layers)]).astype(F32)
    total = total + product_call(got[-1], t, F32)
    return lax.dynamic_update_slice(base, (total * inverse)[None], (STEPS - 1, 0, 0))


def solution(mesh):
    return jax.shard_map(
        per_device,
        mesh=mesh,
        in_specs=(
            P(("groups", "blk"), "layer", None),
            P(("groups", "blk"), "layer", None),
            P("layer", None),
            P("groups", None),
        ),
        out_specs=P(None, "layer", ("groups", "blk")),
        check_vma=False,
    )
```

```python
import functools

import jax
import jax.numpy as jnp
from jax import lax
from jax.experimental import pallas as pl
from jax.experimental.pallas import tpu as pltpu
from jax.sharding import PartitionSpec as P

STEPS = 3
PART = 1024
EXTRA = 8
F32, BF16 = jnp.float32, jnp.bfloat16
VMEM = pl.BlockSpec(memory_space=pltpu.VMEM)
SMEM = pl.BlockSpec(memory_space=pltpu.SMEM)


def after(x, *earlier):
    return lax.optimization_barrier((x,) + earlier)[0]


def dot(x, y, contract):
    return lax.dot_general(x, y, (contract, ((), ())), preferred_element_type=F32)


def added(refs):
    total = refs[0][...].astype(F32)
    for ref in refs[1:]:
        total = total + ref[...].astype(F32)
    return total


def choose(column, p):
    hot = one_hot(column, p.shape[0])
    total = None
    for _ in range(3):
        term = p.astype(BF16)
        p = p - term.astype(F32)
        part = dot(hot, term, ((1,), (0,)))
        total = part if total is None else total + part
    return total


def weights_of(eig_ref, columns):
    return 1.0 / (eig_ref[:, columns] + 0.05)


def one_hot(column, length):
    shape = (column.shape[0], length)
    return (lax.broadcasted_iota(jnp.int32, shape, 1) == column).astype(F32).astype(BF16)


def scores_kernel(steps, first, layers, me_ref, *refs):
    x_refs, refs = [], refs
    for _, n in steps:
        x_refs.append(refs[:n])
        refs = refs[n:]
    (t_ref, eig_ref, order_ref), refs = refs[:3], refs[3:]
    outs, acc = refs[:layers], refs[layers]
    p, squares = [None] * len(steps), None
    for c in range(0, t_ref.shape[1], PART):
        columns = slice(c, c + PART)
        weights = weights_of(eig_ref, columns)
        t = t_ref[:, columns]
        for i, group in enumerate(x_refs):
            x = (added([ref.at[:, columns] for ref in group]) * weights).astype(BF16)
            part = dot(x, t, ((1,), (1,)))
            p[i] = part if p[i] is None else p[i] + part
        if first:
            tf = t.astype(F32)
            square = tf * tf * weights
            for k in range(0, PART, 128):
                part = square[:, k : k + 128]
                squares = part if squares is None else squares + part
    own = acc.shape[0] // layers
    for i, (step, _) in enumerate(steps):
        acc[...] = choose(order_ref[:, step : step + 1], p[i])
        for by in range(layers):
            start = pl.multiple_of((me_ref[0] ^ by) * own, own)
            outs[by][i * own : (i + 1) * own] = acc[pl.ds(start, own)].astype(outs[by].dtype)
    if first:
        extra = jnp.broadcast_to(jnp.sum(squares.T, axis=0, keepdims=True), (EXTRA, acc.shape[1]))
        for by in range(layers):
            outs[by][len(steps) * own :] = extra


def scores_call(steps, first, layers, me, xs, t, eig, order, sent):
    rows, depth = t.shape
    queries = xs[0].shape[0]
    share = len(steps) * (queries // layers) + (EXTRA if first else 0)
    return pl.pallas_call(
        functools.partial(scores_kernel, steps, first, layers),
        in_specs=[SMEM] + [VMEM] * (len(xs) + 3),
        out_specs=[VMEM] * layers,
        scratch_shapes=[pltpu.VMEM((queries, rows), F32)],
        out_shape=[jax.ShapeDtypeStruct((share, rows), F32 if by == 0 else sent) for by in range(layers)],
        compiler_params=pltpu.CompilerParams(vmem_limit_bytes=12 << 20),
        cost_estimate=pl.CostEstimate(
            flops=2 * len(steps) * queries * rows * depth, bytes_accessed=4 * queries * depth, transcendentals=0
        ),
        name="scores_" + "_".join(str(step) for step, _ in steps),
    )(me, *xs, t, eig, order)


def ordered_kernel(step, layers, me_ref, q_ref, eig_ref, order_ref, *refs):
    outs, hot = refs[:layers], refs[layers]
    queries = q_ref.shape[0]
    own = queries // layers
    for by in range(layers):
        start = pl.multiple_of((me_ref[0] ^ by) * own, own)
        hot[by * own : (by + 1) * own] = one_hot(order_ref[pl.ds(start, own), step : step + 1], queries)
    for c in range(0, q_ref.shape[1], PART):
        columns = slice(c, c + PART)
        x = (q_ref[:, columns].astype(F32) * weights_of(eig_ref, columns)).astype(BF16)
        x = dot(hot[...], x, ((1,), (0,))).astype(BF16)
        for by in range(layers):
            outs[by][:, columns] = x[by * own : (by + 1) * own]


def ordered_call(step, layers, me, q, eig, order):
    queries, depth = q.shape
    return pl.pallas_call(
        functools.partial(ordered_kernel, step, layers),
        in_specs=[SMEM] + [VMEM] * 3,
        out_specs=[VMEM] * layers,
        scratch_shapes=[pltpu.VMEM((queries, queries), BF16)],
        out_shape=[jax.ShapeDtypeStruct((queries // layers, depth), BF16)] * layers,
        compiler_params=pltpu.CompilerParams(vmem_limit_bytes=16 << 20),
        cost_estimate=pl.CostEstimate(
            flops=2 * queries * queries * depth, bytes_accessed=4 * queries * depth, transcendentals=0
        ),
        name="ordered",
    )(me, q, eig, order)


def part_kernel(x_ref, t_ref, *refs):
    pieces, out = refs[:-1], refs[-1]
    own = x_ref.shape[0]
    p = dot(x_ref[...], t_ref[...], ((1,), (1,)))
    total = added(pieces)
    out[:-own] = total[:-own].astype(out.dtype)
    out[-own:] = (total[-own:] + p).astype(out.dtype)


def part_call(x, t, pieces, dtype):
    (own, depth), rows = x.shape, t.shape[0]
    return pl.pallas_call(
        part_kernel,
        in_specs=[VMEM] * (2 + len(pieces)),
        out_specs=VMEM,
        out_shape=jax.ShapeDtypeStruct(pieces[0].shape, dtype),
        compiler_params=pltpu.CompilerParams(vmem_limit_bytes=8 << 20),
        cost_estimate=pl.CostEstimate(flops=2 * own * rows * depth, bytes_accessed=2 * rows * depth, transcendentals=0),
        name="part",
    )(x, t, *pieces)


def base_kernel(*refs):
    ins, (out_ref, inverse_ref) = refs[:-2], refs[-2:]
    own = out_ref.shape[1]
    first = added(ins)
    inverse = 1.0 / jnp.sqrt(first[own : own + 1])
    inverse_ref[...] = inverse
    out_ref[0] = first[:own] * inverse
    out_ref[1:] = jnp.zeros_like(out_ref[1:])


def base_call(own, sums):
    rows = sums[0].shape[1]
    return pl.pallas_call(
        base_kernel,
        out_shape=[jax.ShapeDtypeStruct((STEPS, own, rows), F32), jax.ShapeDtypeStruct((1, rows), F32)],
        compiler_params=pltpu.CompilerParams(vmem_limit_bytes=4 << 20),
        name="base",
    )(*sums)


def per_device(train_grads, query_grads, eigenvalues, order):
    rows, queries = train_grads.shape[0], query_grads.shape[0]
    layers, blks = lax.axis_size("layer"), lax.axis_size("blk")
    me = lax.axis_index("layer").astype(jnp.int32).reshape(1)
    t = train_grads.reshape(rows, -1)
    q = query_grads.reshape(queries, -1)
    columns = order.T
    evens = range(0, blks, 2)
    even_on = [(i, (i + 2) % blks) for i in evens]

    def exchange(pieces):
        bys = [1, *range(layers - 1, 1, -1)]
        got = [lax.ppermute(pieces[by], "layer", [(i, i ^ by) for i in range(layers)]) for by in bys]
        return [pieces[0]] + got

    odd_two = lax.ppermute(q, "blk", [(i + 1, (i + 3) % blks) for i in evens])
    pieces = scores_call(((0, 1),), True, layers, me, [q], t, eigenvalues, columns, F32)
    sums0 = exchange(pieces)

    ordered = ordered_call(2, layers, me, after(q, *pieces), eigenvalues, columns)
    bys = [*range(layers - 1, 0, -1), 0]
    parts = [ordered[by] for by in bys]
    odd_one = lax.ppermute(after(q, sums0[1]), "blk", [(i, i + 1) for i in evens])
    odd_two = after(odd_two, parts[0])
    parts[1] = after(parts[1], odd_two)
    parts[2:] = lax.optimization_barrier((*parts[2:], odd_two, *sums0))[: layers - 2]

    even_one = lax.ppermute(odd_two, "blk", [(i + 1, i) for i in evens])
    xs = [odd_one, even_one, odd_two]
    pieces = scores_call(((1, 2), (2, 1)), False, layers, me, xs, t, eigenvalues, columns, F32)
    base, inverse = base_call(queries // layers, sums0)

    parts = [lax.ppermute(part, "blk", even_on) for part in parts]
    got = []
    for by, part in zip(bys[:-1], parts):
        mine = part_call(part, t, [pieces[by]], BF16)
        got.append(lax.ppermute(mine, "layer", [(i, i ^ by) for i in range(layers)]))
    total = part_call(parts[-1], t, [pieces[0], *got[:-1]], F32) + got[-1].astype(F32)
    total = total.reshape(2, queries // layers, rows) * inverse[None]
    return lax.dynamic_update_slice(base, total, (1, 0, 0))


def solution(mesh):
    return jax.shard_map(
        per_device,
        mesh=mesh,
        in_specs=(
            P(("groups", "blk"), "layer", None),
            P(("groups", "blk"), "layer", None),
            P("layer", None),
            P("groups", None),
        ),
        out_specs=P(None, "layer", ("groups", "blk")),
        check_vma=False,
    )
```

```python
import functools

import jax
import jax.numpy as jnp
from jax import lax
from jax.experimental import pallas as pl
from jax.experimental.pallas import tpu as pltpu
from jax.sharding import PartitionSpec as P

STEPS = 3
PART = 1024
EXTRA = 8
F32, BF16 = jnp.float32, jnp.bfloat16
VMEM = pl.BlockSpec(memory_space=pltpu.VMEM)
SMEM = pl.BlockSpec(memory_space=pltpu.SMEM)


def after(x, *earlier):
    return lax.optimization_barrier((x,) + earlier)[0]


def dot(x, y, contract):
    return lax.dot_general(x, y, (contract, ((), ())), preferred_element_type=F32)


def added(refs):
    total = refs[0][...].astype(F32)
    for ref in refs[1:]:
        total = total + ref[...].astype(F32)
    return total


def choose(column, p):
    hot = one_hot(column, p.shape[0])
    total = None
    for _ in range(3):
        term = p.astype(BF16)
        p = p - term.astype(F32)
        part = dot(hot, term, ((1,), (0,)))
        total = part if total is None else total + part
    return total


def weights_of(eig_ref, columns):
    return 1.0 / (eig_ref[:, columns] + 0.05)


def one_hot(column, length):
    shape = (column.shape[0], length)
    return (lax.broadcasted_iota(jnp.int32, shape, 1) == column).astype(F32).astype(BF16)


def scores_kernel(steps, first, layers, me_ref, *refs):
    x_refs, refs = [], refs
    for _, n in steps:
        x_refs.append(refs[:n])
        refs = refs[n:]
    (t_ref, eig_ref, order_ref), refs = refs[:3], refs[3:]
    outs, acc = refs[:layers], refs[layers]
    p, squares = [None] * len(steps), None
    for c in range(0, t_ref.shape[1], PART):
        columns = slice(c, c + PART)
        weights = weights_of(eig_ref, columns)
        t = t_ref[:, columns]
        for i, group in enumerate(x_refs):
            x = (added([ref.at[:, columns] for ref in group]) * weights).astype(BF16)
            part = dot(x, t, ((1,), (1,)))
            p[i] = part if p[i] is None else p[i] + part
        if first:
            tf = t.astype(F32)
            square = tf * tf * weights
            for k in range(0, PART, 128):
                part = square[:, k : k + 128]
                squares = part if squares is None else squares + part
    own = acc.shape[0] // layers
    for i, (step, _) in enumerate(steps):
        acc[...] = choose(order_ref[:, step : step + 1], p[i])
        for by in range(layers):
            start = pl.multiple_of((me_ref[0] ^ by) * own, own)
            outs[by][i * own : (i + 1) * own] = acc[pl.ds(start, own)].astype(outs[by].dtype)
    if first:
        extra = jnp.broadcast_to(jnp.sum(squares.T, axis=0, keepdims=True), (EXTRA, acc.shape[1]))
        for by in range(layers):
            outs[by][len(steps) * own :] = extra


def scores_call(steps, first, layers, me, xs, t, eig, order, sent):
    rows, depth = t.shape
    queries = xs[0].shape[0]
    share = len(steps) * (queries // layers) + (EXTRA if first else 0)
    return pl.pallas_call(
        functools.partial(scores_kernel, steps, first, layers),
        in_specs=[SMEM] + [VMEM] * (len(xs) + 3),
        out_specs=[VMEM] * layers,
        scratch_shapes=[pltpu.VMEM((queries, rows), F32)],
        out_shape=[jax.ShapeDtypeStruct((share, rows), F32 if by == 0 else sent) for by in range(layers)],
        compiler_params=pltpu.CompilerParams(vmem_limit_bytes=12 << 20),
        cost_estimate=pl.CostEstimate(
            flops=2 * len(steps) * queries * rows * depth, bytes_accessed=4 * queries * depth, transcendentals=0
        ),
        name="scores_" + "_".join(str(step) for step, _ in steps),
    )(me, *xs, t, eig, order)


def ordered_kernel(step, layers, me_ref, q_ref, eig_ref, order_ref, *refs):
    outs, hot = refs[:layers], refs[layers]
    queries = q_ref.shape[0]
    own = queries // layers
    for by in range(layers):
        start = pl.multiple_of((me_ref[0] ^ by) * own, own)
        hot[by * own : (by + 1) * own] = one_hot(order_ref[pl.ds(start, own), step : step + 1], queries)
    for c in range(0, q_ref.shape[1], PART):
        columns = slice(c, c + PART)
        x = (q_ref[:, columns].astype(F32) * weights_of(eig_ref, columns)).astype(BF16)
        x = dot(hot[...], x, ((1,), (0,))).astype(BF16)
        for by in range(layers):
            outs[by][:, columns] = x[by * own : (by + 1) * own]


def ordered_call(step, layers, me, q, eig, order):
    queries, depth = q.shape
    return pl.pallas_call(
        functools.partial(ordered_kernel, step, layers),
        in_specs=[SMEM] + [VMEM] * 3,
        out_specs=[VMEM] * layers,
        scratch_shapes=[pltpu.VMEM((queries, queries), BF16)],
        out_shape=[jax.ShapeDtypeStruct((queries // layers, depth), BF16)] * layers,
        compiler_params=pltpu.CompilerParams(vmem_limit_bytes=16 << 20),
        cost_estimate=pl.CostEstimate(
            flops=2 * queries * queries * depth, bytes_accessed=4 * queries * depth, transcendentals=0
        ),
        name="ordered",
    )(me, q, eig, order)


def part_kernel(x_ref, t_ref, *refs):
    pieces, out = refs[:-1], refs[-1]
    own = x_ref.shape[0]
    p = dot(x_ref[...], t_ref[...], ((1,), (1,)))
    total = added(pieces)
    out[:-own] = total[:-own].astype(out.dtype)
    out[-own:] = (total[-own:] + p).astype(out.dtype)


def part_call(x, t, pieces, dtype):
    (own, depth), rows = x.shape, t.shape[0]
    return pl.pallas_call(
        part_kernel,
        in_specs=[VMEM] * (2 + len(pieces)),
        out_specs=VMEM,
        out_shape=jax.ShapeDtypeStruct(pieces[0].shape, dtype),
        compiler_params=pltpu.CompilerParams(vmem_limit_bytes=8 << 20),
        cost_estimate=pl.CostEstimate(flops=2 * own * rows * depth, bytes_accessed=2 * rows * depth, transcendentals=0),
        name="part",
    )(x, t, *pieces)


def base_kernel(*refs):
    ins, (out_ref, inverse_ref) = refs[:-2], refs[-2:]
    own = out_ref.shape[1]
    first = added(ins)
    inverse = 1.0 / jnp.sqrt(first[own : own + 1])
    inverse_ref[...] = inverse
    out_ref[0] = first[:own] * inverse
    out_ref[1:] = jnp.zeros_like(out_ref[1:])


def base_call(own, sums):
    rows = sums[0].shape[1]
    return pl.pallas_call(
        base_kernel,
        out_shape=[jax.ShapeDtypeStruct((STEPS, own, rows), F32), jax.ShapeDtypeStruct((1, rows), F32)],
        compiler_params=pltpu.CompilerParams(vmem_limit_bytes=4 << 20),
        name="base",
    )(*sums)


def per_device(train_grads, query_grads, eigenvalues, order):
    rows, queries = train_grads.shape[0], query_grads.shape[0]
    layers, blks = lax.axis_size("layer"), lax.axis_size("blk")
    me = lax.axis_index("layer").astype(jnp.int32).reshape(1)
    t = train_grads.reshape(rows, -1)
    q = query_grads.reshape(queries, -1)
    columns = order.T
    evens = range(0, blks, 2)
    even_on = [(i, (i + 2) % blks) for i in evens]

    def exchange(pieces):
        bys = [1, *range(layers - 1, 1, -1)]
        got = [lax.ppermute(pieces[by], "layer", [(i, i ^ by) for i in range(layers)]) for by in bys]
        return [pieces[0]] + got

    odd_two = lax.ppermute(q, "blk", [(i + 1, (i + 3) % blks) for i in evens])
    pieces = scores_call(((0, 1),), True, layers, me, [q], t, eigenvalues, columns, F32)
    sums0 = exchange(pieces)

    ordered = ordered_call(2, layers, me, after(q, *pieces), eigenvalues, columns)
    bys = [*range(layers - 1, 0, -1), 0]
    parts = [ordered[by] for by in bys]
    odd_one = lax.ppermute(after(q, *pieces), "blk", [(i, i + 1) for i in evens])
    odd_two = after(odd_two, parts[0], sums0[1])
    parts[1] = after(parts[1], odd_two)
    parts[2:] = lax.optimization_barrier((*parts[2:], odd_two, *sums0))[: layers - 2]

    even_one = lax.ppermute(odd_two, "blk", [(i + 1, i) for i in evens])
    xs = [odd_one, even_one, odd_two]
    pieces = scores_call(((1, 2), (2, 1)), False, layers, me, xs, t, eigenvalues, columns, F32)
    base, inverse = base_call(queries // layers, sums0)

    parts = [lax.ppermute(part, "blk", even_on) for part in parts]
    got = []
    for by, part in zip(bys[:-1], parts):
        mine = part_call(part, t, [pieces[by]], BF16)
        got.append(lax.ppermute(mine, "layer", [(i, i ^ by) for i in range(layers)]))
    total = part_call(parts[-1], t, [pieces[0], *got[:-1]], F32) + got[-1].astype(F32)
    total = total.reshape(2, queries // layers, rows) * inverse[None]
    return lax.dynamic_update_slice(base, total, (1, 0, 0))


def solution(mesh):
    return jax.shard_map(
        per_device,
        mesh=mesh,
        in_specs=(
            P(("groups", "blk"), "layer", None),
            P(("groups", "blk"), "layer", None),
            P("layer", None),
            P("groups", None),
        ),
        out_specs=P(None, "layer", ("groups", "blk")),
        check_vma=False,
    )
```
